256 devices in a mesh: ia: 16 (over z_hi, y, core), ja: 4 (over x), ka: 4 (over z_lo).
Axes of the slice: x: 4, y: 4, z: 8 (z_hi: 2, z_lo: 4; z = z_hi * 4 + z_lo), core: 2. Of those that a mesh axis runs over, the one named last changes fastest.
Arguments:
- tensor: float32 [256, 256, 8192], P('ia', 'ka', 'ja'), may hold values from -6 to 6
- factor_b: float32 [8192, 64], P(('ja', 'ka')), may hold values from -1 to 1
- factor_c: float32 [256, 64], P('ka'), may hold values from -1 to 1
Outputs:
- factor_a: float32 [256, 64], P(('ia', 'ja', 'ka'))
- mode_two: float32 [64, 4, 2048], P(None, 'ja', ('ia', 'ka'))
The draws below stay inside these ranges and needn't reach their ends.
All inputs are finite; a program needn't handle non-finite values.
Results may differ from the reference program's by a relative error of at most 0.00026.
Values sent between devices are 32-bit elements; how exact they have to be, the bound alone decides.
A program may use at most 64 MiB of HBM per device.

```python
import jax
import jax.numpy as jnp
from jax import lax

R = 64
J_DEV = 2048
I = 256
J = 8192
K = 256
N_JA = 4


def common_factor(key, row_total):
    first_key, second_key = jax.random.split(key, 2)
    shared = jax.random.normal(first_key, (row_total, 1), jnp.float32)
    noise = jax.random.normal(second_key, (row_total, R), jnp.float32)
    values = jnp.clip(shared + noise, -8.0, 8.0) / jnp.sqrt(jnp.float32(row_total))
    return jnp.clip(values, -1.0, 1.0)


def draw_factor_b(key, part):
    return common_factor(jax.random.fold_in(key, 11), J)


def draw_factor_c(key, part):
    return common_factor(jax.random.fold_in(key, 23), K)


def level_of(own_key, extent, cuts, smallest, largest):
    factor_of, own = 1.0, jax.random.fold_in(own_key, 6)
    for axis_at, blocks in cuts:
        steps = jnp.exp(jax.random.uniform(jax.random.fold_in(own, axis_at), (blocks,), jnp.float32, smallest / len(cuts), largest / len(cuts)))
        factor_of = factor_of * jnp.repeat(steps, extent[axis_at] // blocks).reshape([-1 if axis == axis_at else 1 for axis in range(len(extent))])
    return factor_of


def scatter_about(own_key, extent, deviation, most, cuts=(), kind=jnp.bfloat16):
    result = deviation * jax.random.normal(own_key, extent, jnp.float32)
    if cuts:
        result = result * level_of(own_key, extent, cuts, -0.22, 0.18)
    return jnp.clip(result, -most, most).astype(kind)


def setup_inputs(seed: int = 0) -> dict:
    key_list = jax.random.split(jax.random.key(seed), 4)
    return {
        "tensor": scatter_about(key_list[0], (I, K, J), 1.0, 6.0, ((0, 16), (1, 4), (2, 4)), jnp.float32),
        "factor_b": draw_factor_b(jax.random.fold_in(key_list[3], 71), 0),
        "factor_c": draw_factor_c(jax.random.fold_in(key_list[3], 71), 0),
    }


def reference(tensor, factor_b, factor_c):
    highest = lax.Precision.HIGHEST
    gram_b = jnp.dot(factor_b.T.astype(jnp.float32), factor_b.astype(jnp.float32), precision=highest, preferred_element_type=jnp.float32)
    gram_c = jnp.dot(factor_c.T.astype(jnp.float32), factor_c.astype(jnp.float32), precision=highest, preferred_element_type=jnp.float32)
    triangle = jnp.linalg.cholesky(gram_b * gram_c)

    def mode_one_row(snapshot_rows):
        contracted = jnp.dot(factor_c.T.astype(jnp.float32), snapshot_rows.astype(jnp.float32), precision=highest, preferred_element_type=jnp.float32)
        return jnp.sum(contracted * factor_b.T, axis=1)
    mode_one = lax.map(mode_one_row, tensor)
    factor_a = jax.scipy.linalg.cho_solve((triangle, True), mode_one.T).T

    def accumulate(running, scan_items):
        snapshot_rows, a_row = scan_items
        contracted = jnp.dot(factor_c.T.astype(jnp.float32), snapshot_rows.astype(jnp.float32), precision=highest, preferred_element_type=jnp.float32)
        return (running + contracted * a_row[:, None], None)
    empty_sum = jnp.zeros((factor_c.shape[1], tensor.shape[2]), jnp.float32)
    mode_two, _ = lax.scan(accumulate, empty_sum, (tensor, factor_a))
    return (factor_a, mode_two.reshape(factor_c.shape[1], N_JA, J_DEV))
```

```python
import jax
import jax.numpy as jnp
from jax import lax
from jax.experimental import pallas as pl
from jax.experimental.pallas import tpu as pltpu
from jax.sharding import PartitionSpec as P

MESH = pl.DeviceIdType.MESH
F32 = jnp.float32
BF16 = jnp.bfloat16
HIGHEST = lax.Precision.HIGHEST

R = 64
NI = 16
NK = 64
NT = 16
LANES = 128
NX, NY, NZ, NZLO = 4, 4, 8, 4
EARLY = 4
MIDDLE = 10


def place(x, y, z, core):
    return (((z // NZLO) * NY + y) * 2 + core, x, z % NZLO)


def kernel(
    tensor,
    b_ref,
    c_ref,
    a_out,
    two_out,
    rows,
    partial,
    c_wide,
    gram_own,
    gram_x,
    gram_mid,
    gram_z,
    b_near,
    b_far,
    one_acc,
    one_own,
    one_recv,
    h_inv,
    a_wide,
    a_rows,
    pair_send,
    pair_recv,
    packed,
    two_recv,
    t_sem,
    b_send,
    b_recv_sem,
    gx_send,
    gx_recv,
    gz_send,
    gz_recv,
    one_send,
    one_recv_sem,
    pair_ssem,
    pair_rsem,
    two_send,
    two_recv_sem,
):
    ia = lax.axis_index("ia")
    x = lax.axis_index("ja")
    zlo = lax.axis_index("ka")
    core = ia % 2
    y = (ia // 2) % NY
    zhi = ia // (2 * NY)
    z = zhi * NZLO + zlo

    def at_z(d):
        return place(x, y, (z + d + NZ) % NZ, core)

    def at_x(d):
        return place((x + d) % NX, y, z, core)

    other_core = place(x, y, z, 1 - core)

    def remote(src, dst, send, recv, target):
        copy = pltpu.make_async_remote_copy(
            src_ref=src, dst_ref=dst, send_sem=send, recv_sem=recv, device_id=target, device_id_type=MESH
        )
        return copy

    def load_row(i):
        return pltpu.make_async_copy(tensor.at[i], rows.at[i], t_sem.at[i])

    for i in range(NI):
        load_row(i).start()

    barrier = pltpu.get_barrier_semaphore()
    peers = [other_core]
    peers += [at_x(d) for d in range(1, NX)]
    peers += [place(x, (y + d) % NY, z, core) for d in range(1, NY)]
    peers += [at_z(d) for d in range(1, NZ)]
    for peer in peers:
        pl.semaphore_signal(barrier, inc=1, device_id=peer, device_id_type=MESH)

    c_t = c_ref[...].T
    c_hi = c_t.astype(BF16)
    c_lo = (c_t - c_hi.astype(F32)).astype(BF16)
    c_wide[...] = jnp.concatenate([c_hi, c_lo, c_hi, c_lo], axis=1)
    b_own = b_ref[...]
    gram_b = lax.dot_general(b_own, b_own, (((1,), (1,)), ((), ())), precision=HIGHEST, preferred_element_type=F32)
    gram_c = lax.dot_general(c_t, c_t, (((1,), (1,)), ((), ())), precision=HIGHEST, preferred_element_type=F32)
    gram_own[...] = jnp.concatenate([gram_b, gram_c], axis=1)

    def contract(i, carry):
        load_row(i).wait()
        for chunk in range(4):
            values = rows[i, :, pl.ds(chunk * 512, 512)]
            hi = values.astype(BF16)
            lo = (values - hi.astype(F32)).astype(BF16)
            out = jnp.dot(c_wide[...], jnp.concatenate([hi, hi, lo, lo], axis=0), preferred_element_type=F32)
            for part in range(4):
                partial[chunk * 4 + part, i] = out[:, part * LANES : (part + 1) * LANES]
        return carry

    lax.fori_loop(0, EARLY, contract, 0)

    pl.semaphore_wait(barrier, len(peers))

    half = b_ref.shape[1] // 2
    b_copies = [
        remote(b_ref.at[:, pl.ds(0, half)], b_far.at[0], b_send.at[2], b_recv_sem.at[2], at_z(2)),
        remote(b_ref.at[:, pl.ds(half, half)], b_far.at[1], b_send.at[3], b_recv_sem.at[3], at_z(-2)),
        remote(b_ref, b_near.at[0], b_send.at[0], b_recv_sem.at[0], at_z(1)),
        remote(b_ref, b_near.at[1], b_send.at[1], b_recv_sem.at[1], at_z(-1)),
    ]
    gx_copies = [remote(gram_own, gram_x.at[d - 1], gx_send.at[d - 1], gx_recv.at[d - 1], at_x(d)) for d in range(1, NX)]
    for copy in gx_copies + b_copies:
        copy.start()

    lax.fori_loop(EARLY, MIDDLE, contract, 0)

    for copy in gx_copies:
        copy.wait_recv()
    own = gram_own[...]
    total = own + gram_x[0] + gram_x[1] + gram_x[2]
    lane = lax.broadcasted_iota(jnp.int32, (R, LANES), 1)
    gram_mid[...] = jnp.where(lane < R, total, own)
    gz_copies = [
        remote(gram_mid, gram_z.at[n], gz_send.at[n], gz_recv.at[n], at_z(d)) for n, d in enumerate((2, 1, -1))
    ]
    for copy in gz_copies:
        copy.start()

    lax.fori_loop(MIDDLE, NI, contract, 0)

    def first_block(i, carry):
        acc = jnp.zeros((R, LANES), F32)
        for part in range(4):
            acc += partial[zlo * 4 + part, i] * b_ref[:, part * LANES : (part + 1) * LANES]
        one_acc[i] = acc
        return carry

    lax.fori_loop(0, NI, first_block, 0)

    b_copies[2].wait_recv()
    b_copies[3].wait_recv()
    before = (zlo + 3) % NZLO
    after = (zlo + 1) % NZLO
    across = (zlo + 2) % NZLO

    def near_blocks(i, carry):
        acc = one_acc[i]
        for part in range(4):
            acc += partial[before * 4 + part, i] * b_near[0, :, part * LANES : (part + 1) * LANES]
            acc += partial[after * 4 + part, i] * b_near[1, :, part * LANES : (part + 1) * LANES]
        one_acc[i] = acc
        return carry

    lax.fori_loop(0, NI, near_blocks, 0)

    b_copies[0].wait_recv()
    b_copies[1].wait_recv()
    lane8 = lax.broadcasted_iota(jnp.int32, (8, LANES), 1)

    def far_block(i, carry):
        acc = one_acc[i]
        for part in range(4):
            acc += (
                partial[across * 4 + part, i]
                * b_far[part // 2, :, (part % 2) * LANES : (part % 2 + 1) * LANES]
            )
        for g in range(8):
            total = jnp.sum(acc[g * 8 : (g + 1) * 8], axis=1, keepdims=True)
            carry = jnp.where(lane8 == g * NI + i, total, carry)
        return carry

    one_own[...] = lax.fori_loop(0, NI, far_block, jnp.zeros((8, LANES), F32))

    one_targets = [((3 - n // NZLO), (3 - n % NZLO)) for n in range(NX * NZLO - 1)]
    for n, (dx, dz) in enumerate(one_targets):
        target = place((x + dx) % NX, y, zhi * NZLO + (zlo + dz) % NZLO, core)
        remote(one_own, one_recv.at[n], one_send, one_recv_sem, target).start()

    for copy in gz_copies:
        copy.wait_recv()
    grams = gram_mid[...] + gram_z[0] + gram_z[1] + gram_z[2]
    product = grams * pltpu.roll(grams, R, 1)
    row_id = lax.broadcasted_iota(jnp.int32, (R, LANES), 0)
    work = jnp.where(lane < R, product, jnp.where(lane == row_id + R, 1.0, 0.0))
    groups = [work[g * 8 : (g + 1) * 8] for g in range(8)]
    sub = lax.broadcasted_iota(jnp.int32, (8, LANES), 0)
    for p in range(R):
        gp, s = p // 8, p % 8
        row = groups[gp][s : s + 1]
        scale = lax.rsqrt(row[:, p : p + 1])
        unit = row * scale
        for g in range(gp, 8):
            column = groups[g][:, p : p + 1] * scale
            update = groups[g] - column * unit
            if g == gp:
                update = jnp.where(sub > s, update, jnp.where(sub == s, unit, groups[g]))
            groups[g] = update
    lower_inv = jnp.concatenate(groups, axis=0)[:, R:]
    h_inv[...] = lax.dot_general(
        lower_inv, lower_inv, (((0,), (0,)), ((), ())), precision=HIGHEST, preferred_element_type=F32
    )

    pltpu.make_async_copy(one_recv, one_recv, one_recv_sem).wait()
    mode_one = one_own[...]
    for n in range(NX * NZLO - 1):
        mode_one = mode_one + one_recv[n]
    mode_one_t = jnp.concatenate(
        [mode_one if g == 0 else pltpu.roll(mode_one, LANES - g * NI, 1) for g in range(8)], axis=0
    )
    a_t = jnp.dot(h_inv[...], mode_one_t, precision=HIGHEST, preferred_element_type=F32)
    for i in range(NI):
        a_wide[i] = jnp.broadcast_to(a_t[:, i : i + 1], (R, LANES))

    def combine(tile):
        acc = partial[tile, 0] * a_wide[0]
        for i in range(1, NI):
            acc += partial[tile, i] * a_wide[i]
        return acc

    def block_of(n):
        return ((zhi + 1 + n // NY) % 2, (y + 2 + n) % NY)

    def pair_copy(n):
        return remote(pair_send.at[n], pair_recv.at[n], pair_ssem.at[n], pair_rsem.at[n], other_core)

    def for_other_core(n, carry):
        to_zhi, to_y = block_of(n)
        pair_send[n] = combine((to_zhi * NY + to_y) * 2 + 1 - core)
        pair_copy(n).start()
        return carry

    lax.fori_loop(0, 8, for_other_core, 0)

    lane16 = lax.broadcasted_iota(jnp.int32, (16, LANES), 1) // 32

    def reduce_pair(n):
        to_zhi, to_y = block_of(n)
        value = combine((to_zhi * NY + to_y) * 2 + core)
        pair_copy(n).wait_recv()
        value = value + pair_recv[n]
        for to_zlo in range(NZLO):
            block = value[0:16] if to_zlo == 0 else pltpu.roll(value[0:16], LANES - 32 * to_zlo, 1)
            for g in range(1, 4):
                piece = value[g * 16 : (g + 1) * 16]
                shift = (32 * (g - to_zlo)) % LANES
                block = jnp.where(lane16 == g, pltpu.roll(piece, shift, 1) if shift else piece, block)
            packed[n, to_zlo] = block

    def send_block(n, step):
        to_zhi, to_y = block_of(n)
        to_zlo = (zlo + step) % NZLO
        slot = n * NZLO + step - 1
        remote(
            packed.at[n, to_zlo],
            two_recv.at[slot],
            two_send,
            two_recv_sem,
            place(x, to_y, to_zhi * NZLO + to_zlo, core),
        ).start()

    def far_blocks(n, carry):
        reduce_pair(n)
        for step in (2, 1, 3, 4):
            send_block(n, step)
        return carry

    lax.fori_loop(0, 6, far_blocks, 0)
    lax.fori_loop(7, 8, far_blocks, 0)
    reduce_pair(6)
    for step in (2, 1, 3):
        send_block(6, step)

    a_rows[...] = a_t.T
    a_out[...] = a_rows[pl.ds(x * NZLO + zlo, 1), :]

    two_recv[6 * NZLO + 3] = packed[6, zlo]
    pltpu.make_async_copy(two_recv.at[pl.ds(0, 31)], two_recv.at[pl.ds(0, 31)], two_recv_sem).wait()

    def add_block(n, acc):
        return acc + two_recv[n]

    total = lax.fori_loop(0, 32, add_block, jnp.zeros((16, LANES), F32))
    columns = jnp.concatenate([total if g == 0 else pltpu.roll(total, LANES - 32 * g, 1) for g in range(4)], axis=0)
    two_out[...] = columns.T[0:32]

    for copy in b_copies + gx_copies + gz_copies:
        copy.wait_send()
    pltpu.make_async_copy(one_recv, one_recv, one_send).wait()

    def pair_done(n, carry):
        pair_copy(n).wait_send()
        return carry

    lax.fori_loop(0, 8, pair_done, 0)
    pltpu.make_async_copy(two_recv.at[pl.ds(0, 31)], two_recv.at[pl.ds(0, 31)], two_send).wait()


def body(tensor, factor_b, factor_c):
    dma = pltpu.SemaphoreType.DMA
    vmem = pl.BlockSpec(memory_space=pltpu.VMEM)
    a_rows, two = pl.pallas_call(
        kernel,
        name="cp_step",
        out_shape=(jax.ShapeDtypeStruct((1, R), F32), jax.ShapeDtypeStruct((32, R), F32)),
        in_specs=[pl.BlockSpec(memory_space=pltpu.HBM), vmem, vmem],
        out_specs=(vmem, vmem),
        scratch_shapes=[
            pltpu.VMEM((NI, NK, NT * LANES), F32),
            pltpu.VMEM((NT, NI, R, LANES), F32),
            pltpu.VMEM((R, 4 * NK), BF16),
            pltpu.VMEM((R, LANES), F32),
            pltpu.VMEM((3, R, LANES), F32),
            pltpu.VMEM((R, LANES), F32),
            pltpu.VMEM((3, R, LANES), F32),
            pltpu.VMEM((2, R, 512), F32),
            pltpu.VMEM((2, R, 256), F32),
            pltpu.VMEM((NI, R, LANES), F32),
            pltpu.VMEM((8, LANES), F32),
            pltpu.VMEM((15, 8, LANES), F32),
            pltpu.VMEM((R, R), F32),
            pltpu.VMEM((NI, R, LANES), F32),
            pltpu.VMEM((LANES, R), F32),
            pltpu.VMEM((8, R, LANES), F32),
            pltpu.VMEM((8, R, LANES), F32),
            pltpu.VMEM((8, NZLO, 16, LANES), F32),
            pltpu.VMEM((32, 16, LANES), F32),
            dma((NI,)),
            dma((4,)),
            dma((4,)),
            dma((3,)),
            dma((3,)),
            dma((3,)),
            dma((3,)),
            dma,
            dma,
            dma((8,)),
            dma((8,)),
            dma,
            dma,
        ],
        compiler_params=pltpu.CompilerParams(collective_id=0, has_side_effects=True, vmem_limit_bytes=48 * 2**20),
        cost_estimate=pl.CostEstimate(flops=2**30, bytes_accessed=2**23, transcendentals=0),
    )(tensor, factor_b.T, factor_c)
    return a_rows, two.T.reshape(R, 1, 32)


def solution(mesh):
    placed = (P("ia", "ka", "ja"), P(("ja", "ka"), None), P("ka", None))
    return jax.shard_map(
        body,
        mesh=mesh,
        in_specs=placed,
        out_specs=(P(("ia", "ja", "ka"), None), P(None, "ja", ("ia", "ka"))),
        check_vma=False,
    )
```

```python
import jax
import jax.numpy as jnp
from jax import lax
from jax.experimental import pallas as pl
from jax.experimental.pallas import tpu as pltpu
from jax.sharding import PartitionSpec as P

MESH = pl.DeviceIdType.MESH
F32 = jnp.float32
BF16 = jnp.bfloat16
HIGHEST = lax.Precision.HIGHEST

R = 64
NI = 16
NK = 64
NT = 16
LANES = 128
NX, NY, NZ, NZLO = 4, 4, 8, 4
WITHIN = 2
NEAR = 2 * WITHIN + 1


def place(x, y, z, core):
    return (((z // NZLO) * NY + y) * 2 + core, x, z % NZLO)


def kernel(
    tensor,
    b_hbm,
    c_hbm,
    a_out,
    two_out,
    b_ref,
    c_ref,
    rows,
    partial,
    c_wide,
    gram_own,
    gram_x,
    gram_mid,
    gram_z,
    b_near,
    b_far,
    one_acc,
    one_own,
    one_recv,
    h_inv,
    a_wide,
    a_rows,
    pair_send,
    pair_recv,
    packed,
    near_recv,
    near_sum,
    last_recv,
    far_recv,
    in_sem,
    t_sem,
    b_send,
    b_recv_sem,
    gx_send,
    gx_recv,
    gz_send,
    gz_recv,
    one_send,
    one_recv_sem,
    pair_ssem,
    pair_rsem,
    near_send,
    near_rsem,
    last_send,
    last_rsem,
    far_send,
    far_rsem,
):
    ia = lax.axis_index("ia")
    x = lax.axis_index("ja")
    zlo = lax.axis_index("ka")
    core = ia % 2
    y = (ia // 2) % NY
    zhi = ia // (2 * NY)
    z = zhi * NZLO + zlo

    def at_z(d):
        return place(x, y, (z + d + NZ) % NZ, core)

    def at_x(d):
        return place((x + d) % NX, y, z, core)

    other_core = place(x, y, z, 1 - core)

    def remote(src, dst, send, recv, target):
        copy = pltpu.make_async_remote_copy(
            src_ref=src, dst_ref=dst, send_sem=send, recv_sem=recv, device_id=target, device_id_type=MESH
        )
        return copy

    def load_row(i):
        return pltpu.make_async_copy(tensor.at[i], rows.at[i], t_sem.at[i])

    load_c = pltpu.make_async_copy(c_hbm, c_ref, in_sem.at[0])
    load_b = pltpu.make_async_copy(b_hbm, b_ref, in_sem.at[1])
    load_c.start()
    load_b.start()
    for i in range(NI):
        load_row(i).start()

    barrier = pltpu.get_barrier_semaphore()
    peers = [other_core]
    peers += [at_x(d) for d in range(1, NX)]
    peers += [place(x, (y + d) % NY, z, core) for d in range(1, NY)]
    peers += [at_z(d) for d in range(1, NZ)]
    for peer in peers:
        pl.semaphore_signal(barrier, inc=1, device_id=peer, device_id_type=MESH)

    load_c.wait()
    c_t = c_ref[...].T
    c_hi = c_t.astype(BF16)
    c_lo = (c_t - c_hi.astype(F32)).astype(BF16)
    none = jnp.zeros_like(c_hi)
    for n, part in enumerate((c_hi, c_lo)):
        c_wide[n * 2 * R : n * 2 * R + R] = jnp.concatenate([part, part, none, none], axis=1)
        c_wide[n * 2 * R + R : (n + 1) * 2 * R] = jnp.concatenate([none, none, part, part], axis=1)
    def contract(i, carry):
        load_row(2 * i).wait()
        load_row(2 * i + 1).wait()
        for chunk in range(8):
            operand = []
            for n in range(2):
                values = rows[2 * i + n, :, pl.ds(chunk * 256, 256)]
                hi = values.astype(BF16)
                operand += [hi, (values - hi.astype(F32)).astype(BF16)]
            out = jnp.dot(c_wide[...], jnp.concatenate(operand, axis=0), preferred_element_type=F32)
            out = out[: 2 * R] + out[2 * R :]
            for part in range(2):
                for n in range(2):
                    piece = out[n * R : (n + 1) * R, part * LANES : (part + 1) * LANES]
                    partial[chunk * 2 + part, 2 * i + n] = piece
        return carry

    load_b.wait()
    pl.semaphore_wait(barrier, len(peers))

    half = b_ref.shape[1] // 2
    b_copies = [
        remote(b_ref.at[:, pl.ds(0, half)], b_far.at[0], b_send.at[2], b_recv_sem.at[2], at_z(2)),
        remote(b_ref.at[:, pl.ds(half, half)], b_far.at[1], b_send.at[3], b_recv_sem.at[3], at_z(-2)),
        remote(b_ref, b_near.at[0], b_send.at[0], b_recv_sem.at[0], at_z(1)),
        remote(b_ref, b_near.at[1], b_send.at[1], b_recv_sem.at[1], at_z(-1)),
    ]
    for copy in b_copies:
        copy.start()

    b_own = b_ref[...]
    gram_b = lax.dot_general(b_own, b_own, (((1,), (1,)), ((), ())), precision=HIGHEST, preferred_element_type=F32)
    gram_c = lax.dot_general(c_t, c_t, (((1,), (1,)), ((), ())), precision=HIGHEST, preferred_element_type=F32)
    gram_own[...] = jnp.concatenate([gram_b, gram_c], axis=1)

    gx_copies = [remote(gram_own, gram_x.at[d - 1], gx_send.at[d - 1], gx_recv.at[d - 1], at_x(d)) for d in (2, 1, 3)]
    for copy in gx_copies:
        copy.start()

    lax.fori_loop(0, NI // 2, contract, 0)

    for copy in gx_copies:
        copy.wait_recv()
    own = gram_own[...]
    total = own + gram_x[0] + gram_x[1] + gram_x[2]
    lane = lax.broadcasted_iota(jnp.int32, (R, LANES), 1)
    gram_mid[...] = jnp.where(lane < R, total, own)
    gz_copies = [
        remote(gram_mid, gram_z.at[n], gz_send.at[n], gz_recv.at[n], at_z(d)) for n, d in enumerate((2, 1, -1))
    ]
    for copy in gz_copies:
        copy.start()

    def first_block(i, carry):
        acc = jnp.zeros((R, LANES), F32)
        for part in range(4):
            acc += partial[zlo * 4 + part, i] * b_ref[:, part * LANES : (part + 1) * LANES]
        one_acc[i] = acc
        return carry

    lax.fori_loop(0, NI, first_block, 0)

    b_copies[2].wait_recv()
    b_copies[3].wait_recv()
    before = (zlo + 3) % NZLO
    after = (zlo + 1) % NZLO
    across = (zlo + 2) % NZLO

    def near_blocks(i, carry):
        acc = one_acc[i]
        for part in range(4):
            acc += partial[before * 4 + part, i] * b_near[0, :, part * LANES : (part + 1) * LANES]
            acc += partial[after * 4 + part, i] * b_near[1, :, part * LANES : (part + 1) * LANES]
        one_acc[i] = acc
        return carry

    lax.fori_loop(0, NI, near_blocks, 0)

    b_copies[0].wait_recv()
    b_copies[1].wait_recv()
    lane8 = lax.broadcasted_iota(jnp.int32, (8, LANES), 1)

    def far_block(i, carry):
        acc = one_acc[i]
        for part in range(4):
            acc += (
                partial[across * 4 + part, i]
                * b_far[part // 2, :, (part % 2) * LANES : (part % 2 + 1) * LANES]
            )
        for g in range(8):
            total = jnp.sum(acc[g * 8 : (g + 1) * 8], axis=1, keepdims=True)
            carry = jnp.where(lane8 == g * NI + i, total, carry)
        return carry

    one_own[...] = lax.fori_loop(0, NI, far_block, jnp.zeros((8, LANES), F32))

    one_targets = [((3 - n // NZLO), (3 - n % NZLO)) for n in range(NX * NZLO - 1)]
    for n, (dx, dz) in enumerate(one_targets):
        target = place((x + dx) % NX, y, zhi * NZLO + (zlo + dz) % NZLO, core)
        remote(one_own, one_recv.at[n], one_send, one_recv_sem, target).start()

    for copy in gz_copies:
        copy.wait_recv()
    grams = gram_mid[...] + gram_z[0] + gram_z[1] + gram_z[2]
    product = grams * pltpu.roll(grams, R, 1)
    row_id = lax.broadcasted_iota(jnp.int32, (R, LANES), 0)
    work = jnp.where(lane < R, product, jnp.where(lane == row_id + R, 1.0, 0.0))
    groups = [work[g * 8 : (g + 1) * 8] for g in range(8)]

    def wide(value):
        return jnp.broadcast_to(value, (8, LANES))

    sub = lax.broadcasted_iota(jnp.int32, (8, LANES), 0)
    for p in range(8):
        columns = {g: [wide(groups[g][:, p * 8 + j : p * 8 + j + 1]) for j in range(8)] for g in range(p, 8)}
        block = [[wide(columns[p][j][i : i + 1]) for j in range(i + 1)] for i in range(8)]
        scale = []
        for j in range(8):
            scale.append(lax.rsqrt(block[j][j]))
            for i in range(j + 1, 8):
                block[i][j] = block[i][j] * scale[j]
            for i in range(j + 1, 8):
                for k in range(j + 1, i + 1):
                    block[i][k] = block[i][k] - block[i][j] * block[k][j]
        units = []
        for j in range(8):
            unit = wide(groups[p][j : j + 1])
            for k in range(j):
                unit = unit - block[j][k] * units[k]
            units.append(unit * scale[j])
        done = units[0]
        for j in range(1, 8):
            done = jnp.where(sub == j, units[j], done)
        groups[p] = done
        for g in range(p + 1, 8):
            lower = []
            for j in range(8):
                column = columns[g][j]
                for k in range(j):
                    column = column - lower[k] * block[j][k]
                lower.append(column * scale[j])
                groups[g] = groups[g] - lower[j] * units[j]
    lower_inv = jnp.concatenate(groups, axis=0)[:, R:]
    h_inv[...] = lax.dot_general(
        lower_inv, lower_inv, (((0,), (0,)), ((), ())), precision=HIGHEST, preferred_element_type=F32
    )

    pltpu.make_async_copy(one_recv, one_recv, one_recv_sem).wait()
    mode_one = one_own[...]
    for n in range(NX * NZLO - 1):
        mode_one = mode_one + one_recv[n]
    mode_one_t = jnp.concatenate(
        [mode_one if g == 0 else pltpu.roll(mode_one, LANES - g * NI, 1) for g in range(8)], axis=0
    )
    a_t = jnp.dot(h_inv[...], mode_one_t, precision=HIGHEST, preferred_element_type=F32)
    for i in range(NI):
        a_wide[i] = jnp.broadcast_to(a_t[:, i : i + 1], (R, LANES))

    def combine(tiles):
        accs = [partial[tile, 0] * a_wide[0] for tile in tiles]
        for i in range(1, NI):
            wide_a = a_wide[i]
            accs = [acc + partial[tile, i] * wide_a for acc, tile in zip(accs, tiles)]
        return accs

    order = (2, 1, 3, 0)

    def tiles_of(dy, to_core):
        return [(to_zhi * NY + (y + dy) % NY) * 2 + to_core for to_zhi in range(2)]

    pair_copies = [
        remote(pair_send.at[n], pair_recv.at[n], pair_ssem.at[n], pair_rsem.at[n], other_core) for n in range(NY)
    ]
    for n, dy in enumerate(order):
        for to_zhi, value in enumerate(combine(tiles_of(dy, 1 - core))):
            pair_send[n, to_zhi] = value
        pair_copies[n].start()

    lane16 = lax.broadcasted_iota(jnp.int32, (16, LANES), 1) // 32
    near_copies, far_targets = [], []
    for n, dy in enumerate(order):
        values = combine(tiles_of(dy, core))
        pair_copies[n].wait_recv()
        for to_zhi in range(2):
            value = values[to_zhi] + pair_recv[n, to_zhi]
            for to_zlo in range(NZLO):
                block = value[0:16] if to_zlo == 0 else pltpu.roll(value[0:16], LANES - 32 * to_zlo, 1)
                for g in range(1, 4):
                    piece = value[g * 16 : (g + 1) * 16]
                    shift = (32 * (g - to_zlo)) % LANES
                    block = jnp.where(lane16 == g, pltpu.roll(piece, shift, 1) if shift else piece, block)
                packed[dy, (to_zhi * NZLO + to_zlo + WITHIN + NZ - z) % NZ] = block
        if dy:
            near = remote(
                packed.at[dy, pl.ds(0, NEAR)],
                near_recv.at[n],
                near_send.at[n],
                near_rsem.at[n],
                place(x, (y + dy) % NY, z, core),
            )
            near.start()
            near_copies.append(near)
        for e in range(NEAR, NZ):
            slot = n * (NZ - NEAR) + e - NEAR
            target = place(x, (y + dy) % NY, (z + e - WITHIN) % NZ, core)
            remote(packed.at[dy, e], far_recv.at[slot], far_send, far_rsem, target).start()

    a_rows[...] = a_t.T
    a_out[...] = a_rows[pl.ds(x * NZLO + zlo, 1), :]

    for copy in near_copies:
        copy.wait_recv()
    for e in range(NEAR):
        near_sum[e] = packed[0, e] + near_recv[0, e] + near_recv[1, e] + near_recv[2, e]
    last = [e for d in range(WITHIN, 0, -1) for e in (WITHIN + d, WITHIN - d)]
    last_copies = [
        remote(near_sum.at[e], last_recv.at[n], last_send.at[n], last_rsem.at[n], at_z(e - WITHIN))
        for n, e in enumerate(last)
    ]
    for copy in last_copies:
        copy.start()

    total = near_sum[WITHIN]
    pltpu.make_async_copy(far_recv, far_recv, far_rsem).wait()
    for n in range(NY * (NZ - NEAR)):
        total = total + far_recv[n]
    for n, copy in enumerate(last_copies):
        copy.wait_recv()
        total = total + last_recv[n]
    columns = jnp.concatenate([total if g == 0 else pltpu.roll(total, LANES - 32 * g, 1) for g in range(4)], axis=0)
    two_out[...] = columns.T[0:32]

    for copy in b_copies + gx_copies + gz_copies:
        copy.wait_send()
    pltpu.make_async_copy(one_recv, one_recv, one_send).wait()

    for copy in pair_copies + near_copies + last_copies:
        copy.wait_send()
    pltpu.make_async_copy(far_recv, far_recv, far_send).wait()


def body(tensor, factor_b, factor_c):
    dma = pltpu.SemaphoreType.DMA
    vmem = pl.BlockSpec(memory_space=pltpu.VMEM)
    hbm = pl.BlockSpec(memory_space=pltpu.HBM)
    a_rows, two = pl.pallas_call(
        kernel,
        name="cp_step",
        out_shape=(jax.ShapeDtypeStruct((1, R), F32), jax.ShapeDtypeStruct((32, R), F32)),
        in_specs=[hbm, hbm, hbm],
        out_specs=(vmem, vmem),
        scratch_shapes=[
            pltpu.VMEM((R, 512), F32),
            pltpu.VMEM((NK, R), F32),
            pltpu.VMEM((NI, NK, NT * LANES), F32),
            pltpu.VMEM((NT, NI, R, LANES), F32),
            pltpu.VMEM((4 * R, 4 * NK), BF16),
            pltpu.VMEM((R, LANES), F32),
            pltpu.VMEM((3, R, LANES), F32),
            pltpu.VMEM((R, LANES), F32),
            pltpu.VMEM((3, R, LANES), F32),
            pltpu.VMEM((2, R, 512), F32),
            pltpu.VMEM((2, R, 256), F32),
            pltpu.VMEM((NI, R, LANES), F32),
            pltpu.VMEM((8, LANES), F32),
            pltpu.VMEM((15, 8, LANES), F32),
            pltpu.VMEM((R, R), F32),
            pltpu.VMEM((NI, R, LANES), F32),
            pltpu.VMEM((LANES, R), F32),
            pltpu.VMEM((NY, 2, R, LANES), F32),
            pltpu.VMEM((NY, 2, R, LANES), F32),
            pltpu.VMEM((NY, NZ, 16, LANES), F32),
            pltpu.VMEM((NY - 1, NEAR, 16, LANES), F32),
            pltpu.VMEM((NEAR, 16, LANES), F32),
            pltpu.VMEM((NEAR - 1, 16, LANES), F32),
            pltpu.VMEM((NY * (NZ - NEAR), 16, LANES), F32),
            dma((2,)),
            dma((NI,)),
            dma((4,)),
            dma((4,)),
            dma((3,)),
            dma((3,)),
            dma((3,)),
            dma((3,)),
            dma,
            dma,
            dma((NY,)),
            dma((NY,)),
            dma((NY - 1,)),
            dma((NY - 1,)),
            dma((NEAR - 1,)),
            dma((NEAR - 1,)),
            dma,
            dma,
        ],
        compiler_params=pltpu.CompilerParams(collective_id=0, has_side_effects=True, vmem_limit_bytes=48 * 2**20),
        cost_estimate=pl.CostEstimate(flops=2**30, bytes_accessed=2**23, transcendentals=0),
    )(
        tensor,
        pltpu.with_memory_space_constraint(factor_b.T, pltpu.HBM),
        pltpu.with_memory_space_constraint(factor_c, pltpu.HBM),
    )
    return a_rows, two.T.reshape(R, 1, 32)


def solution(mesh):
    placed = (P("ia", "ka", "ja"), P(("ja", "ka"), None), P("ka", None))
    return jax.shard_map(
        body,
        mesh=mesh,
        in_specs=placed,
        out_specs=(P(("ia", "ja", "ka"), None), P(None, "ja", ("ia", "ka"))),
        check_vma=False,
    )
```

```python
import jax
import jax.numpy as jnp
from jax import lax
from jax.experimental import pallas as pl
from jax.experimental.pallas import tpu as pltpu
from jax.sharding import PartitionSpec as P

MESH = pl.DeviceIdType.MESH
F32 = jnp.float32
BF16 = jnp.bfloat16
HIGHEST = lax.Precision.HIGHEST

R = 64
NI = 16
NK = 64
NT = 16
LANES = 128
NX, NY, NZ, NZLO = 4, 4, 8, 4
WITHIN = 2
NEAR = 2 * WITHIN + 1


def place(x, y, z, core):
    return (((z // NZLO) * NY + y) * 2 + core, x, z % NZLO)


def kernel(
    tensor,
    b_hbm,
    c_hbm,
    a_out,
    two_out,
    b_ref,
    c_ref,
    rows,
    partial,
    c_wide,
    gram_own,
    gram_x,
    gram_mid,
    gram_z,
    gram_sum,
    b_in,
    one_acc,
    one_own,
    one_recv,
    h_inv,
    a_wide,
    a_rows,
    pair_send,
    pair_recv,
    packed,
    near_recv,
    near_sum,
    last_recv,
    far_recv,
    in_sem,
    t_sem,
    b_send,
    b_recv_sem,
    gx_send,
    gx_recv,
    gz_send,
    gz_recv,
    gs_send,
    gs_recv,
    one_send,
    one_recv_sem,
    pair_ssem,
    pair_rsem,
    near_send,
    near_rsem,
    last_send,
    last_rsem,
    far_send,
    far_rsem,
):
    ia = lax.axis_index("ia")
    x = lax.axis_index("ja")
    zlo = lax.axis_index("ka")
    core = ia % 2
    y = (ia // 2) % NY
    zhi = ia // (2 * NY)
    z = zhi * NZLO + zlo

    def at_z(d):
        return place(x, y, (z + d + NZ) % NZ, core)

    def at_x(d):
        return place((x + d) % NX, y, z, core)

    other_core = place(x, y, z, 1 - core)

    def remote(src, dst, send, recv, target):
        copy = pltpu.make_async_remote_copy(
            src_ref=src, dst_ref=dst, send_sem=send, recv_sem=recv, device_id=target, device_id_type=MESH
        )
        return copy

    def load_row(i):
        return pltpu.make_async_copy(tensor.at[i], rows.at[i], t_sem.at[i])

    load_c = pltpu.make_async_copy(c_hbm, c_ref, in_sem.at[0])
    load_b = pltpu.make_async_copy(b_hbm, b_ref, in_sem.at[1])
    load_c.start()
    load_b.start()
    for i in range(NI):
        load_row(i).start()

    barrier = pltpu.get_barrier_semaphore()
    peers = [other_core]
    peers += [at_x(d) for d in range(1, NX)]
    peers += [place(x, (y + d) % NY, z, core) for d in range(1, NY)]
    peers += [at_z(d) for d in range(1, NZ)]
    for peer in peers:
        pl.semaphore_signal(barrier, inc=1, device_id=peer, device_id_type=MESH)

    load_c.wait()
    c_t = c_ref[...].T
    c_hi = c_t.astype(BF16)
    c_lo = (c_t - c_hi.astype(F32)).astype(BF16)
    none = jnp.zeros_like(c_hi)
    for n, part in enumerate((c_hi, c_lo)):
        c_wide[n * 2 * R : n * 2 * R + R] = jnp.concatenate([part, part, none, none], axis=1)
        c_wide[n * 2 * R + R : (n + 1) * 2 * R] = jnp.concatenate([none, none, part, part], axis=1)
    def contract(i, carry):
        load_row(2 * i).wait()
        load_row(2 * i + 1).wait()
        for chunk in range(8):
            operand = []
            for n in range(2):
                values = rows[2 * i + n, :, pl.ds(chunk * 256, 256)]
                hi = values.astype(BF16)
                operand += [hi, (values - hi.astype(F32)).astype(BF16)]
            out = jnp.dot(c_wide[...], jnp.concatenate(operand, axis=0), preferred_element_type=F32)
            out = out[: 2 * R] + out[2 * R :]
            for part in range(2):
                for n in range(2):
                    piece = out[n * R : (n + 1) * R, part * LANES : (part + 1) * LANES]
                    partial[chunk * 2 + part, 2 * i + n] = piece
        return carry

    load_b.wait()
    pl.semaphore_wait(barrier, len(peers))

    half = b_ref.shape[1] // 2
    own_half = pl.ds(pl.multiple_of(core * half, half), half)
    quarters = [pl.ds(pl.multiple_of(core * half + n * half // 2, half // 2), half // 2) for n in range(2)]
    far_copies = [
        remote(b_ref.at[:, quarters[n]], b_in.at[2, :, quarters[n]], b_send.at[2 + n], b_recv_sem.at[2 + n], at_z(d))
        for n, d in enumerate((2, -2))
    ]
    near_b_copies = [
        remote(b_ref.at[:, own_half], b_in.at[n, :, own_half], b_send.at[n], b_recv_sem.at[n], at_z(d))
        for n, d in enumerate((1, -1))
    ]
    swap_copies = [
        remote(b_in.at[n, :, own_half], b_in.at[n, :, own_half], b_send.at[4 + n], b_recv_sem.at[4 + n], other_core)
        for n in range(3)
    ]
    b_copies = far_copies + near_b_copies
    for copy in b_copies:
        copy.start()

    b_own = b_ref[...]
    gram_b = lax.dot_general(b_own, b_own, (((1,), (1,)), ((), ())), precision=HIGHEST, preferred_element_type=F32)
    gram_c = lax.dot_general(c_t, c_t, (((1,), (1,)), ((), ())), precision=HIGHEST, preferred_element_type=F32)
    gram_own[...] = jnp.concatenate([gram_b, gram_c], axis=1)

    own_rows = pl.ds(pl.multiple_of(core * (R // 2), R // 2), R // 2)
    gx_copies = [remote(gram_own.at[own_rows], gram_x.at[d - 1], gx_send.at[d - 1], gx_recv.at[d - 1], at_x(d)) for d in (2, 1, 3)]
    for copy in gx_copies:
        copy.start()

    lax.fori_loop(0, NI // 2, contract, 0)

    for copy in gx_copies:
        copy.wait_recv()
    own = gram_own[own_rows, :]
    total = own + gram_x[0] + gram_x[1] + gram_x[2]
    gram_mid[...] = jnp.where(lax.broadcasted_iota(jnp.int32, (R // 2, LANES), 1) < R, total, own)
    gz_copies = [
        remote(gram_mid, gram_z.at[n], gz_send.at[n], gz_recv.at[n], at_z(d)) for n, d in enumerate((2, 1, -1))
    ]
    for copy in gz_copies:
        copy.start()

    def first_block(i, carry):
        acc = jnp.zeros((R, LANES), F32)
        for part in range(4):
            acc += partial[zlo * 4 + part, i] * b_ref[:, part * LANES : (part + 1) * LANES]
        one_acc[i] = acc
        return carry

    lax.fori_loop(0, NI, first_block, 0)

    for copy in far_copies:
        copy.wait_recv()
    swap_copies[2].start()
    for n in range(2):
        near_b_copies[n].wait_recv()
        swap_copies[n].start()
    blocks = ((zlo + 3) % NZLO, (zlo + 1) % NZLO, (zlo + 2) % NZLO)

    def half_blocks(i, to_core):
        acc = one_acc[i]
        for n in range(3):
            for part in range(2):
                start = pl.multiple_of(to_core * half + part * LANES, LANES)
                acc += partial[blocks[n] * 4 + to_core * 2 + part, i] * b_in[n, :, pl.ds(start, LANES)]
        return acc

    def fetched_half(i, carry):
        one_acc[i] = half_blocks(i, core)
        return carry

    lax.fori_loop(0, NI, fetched_half, 0)

    for copy in swap_copies:
        copy.wait_recv()
    lane8 = lax.broadcasted_iota(jnp.int32, (8, LANES), 1)

    def handed_half(i, carry):
        acc = half_blocks(i, 1 - core)
        for g in range(8):
            total = jnp.sum(acc[g * 8 : (g + 1) * 8], axis=1, keepdims=True)
            carry = jnp.where(lane8 == g * NI + i, total, carry)
        return carry

    one_own[...] = lax.fori_loop(0, NI, handed_half, jnp.zeros((8, LANES), F32))

    one_targets = [((3 - n // NZLO), (3 - n % NZLO)) for n in range(NX * NZLO - 1)]
    for n, (dx, dz) in enumerate(one_targets):
        target = place((x + dx) % NX, y, zhi * NZLO + (zlo + dz) % NZLO, core)
        remote(one_own, one_recv.at[n], one_send, one_recv_sem, target).start()

    for copy in gz_copies:
        copy.wait_recv()
    gram_sum[own_rows, :] = gram_mid[...] + gram_z[0] + gram_z[1] + gram_z[2]
    g_swap = remote(gram_sum.at[own_rows], gram_sum.at[own_rows], gs_send, gs_recv, other_core)
    g_swap.start()
    g_swap.wait_recv()
    grams = gram_sum[...]
    lane = lax.broadcasted_iota(jnp.int32, (R, LANES), 1)
    product = grams * pltpu.roll(grams, R, 1)
    row_id = lax.broadcasted_iota(jnp.int32, (R, LANES), 0)
    work = jnp.where(lane < R, product, jnp.where(lane == row_id + R, 1.0, 0.0))
    groups = [work[g * 8 : (g + 1) * 8] for g in range(8)]

    def wide(value):
        return jnp.broadcast_to(value, (8, LANES))

    sub = lax.broadcasted_iota(jnp.int32, (8, LANES), 0)
    for p in range(8):
        columns = {g: [wide(groups[g][:, p * 8 + j : p * 8 + j + 1]) for j in range(8)] for g in range(p, 8)}
        block = [[wide(columns[p][j][i : i + 1]) for j in range(i + 1)] for i in range(8)]
        scale = []
        for j in range(8):
            scale.append(lax.rsqrt(block[j][j]))
            for i in range(j + 1, 8):
                block[i][j] = block[i][j] * scale[j]
            for i in range(j + 1, 8):
                for k in range(j + 1, i + 1):
                    block[i][k] = block[i][k] - block[i][j] * block[k][j]
        units = []
        for j in range(8):
            unit = wide(groups[p][j : j + 1])
            for k in range(j):
                unit = unit - block[j][k] * units[k]
            units.append(unit * scale[j])
        done = units[0]
        for j in range(1, 8):
            done = jnp.where(sub == j, units[j], done)
        groups[p] = done
        for g in range(p + 1, 8):
            lower = []
            for j in range(8):
                column = columns[g][j]
                for k in range(j):
                    column = column - lower[k] * block[j][k]
                lower.append(column * scale[j])
                groups[g] = groups[g] - lower[j] * units[j]
    lower_inv = jnp.concatenate(groups, axis=0)[:, R:]
    h_inv[...] = lax.dot_general(
        lower_inv, lower_inv, (((0,), (0,)), ((), ())), precision=HIGHEST, preferred_element_type=F32
    )

    pltpu.make_async_copy(one_recv, one_recv, one_recv_sem).wait()
    mode_one = one_own[...]
    for n in range(NX * NZLO - 1):
        mode_one = mode_one + one_recv[n]
    mode_one_t = jnp.concatenate(
        [mode_one if g == 0 else pltpu.roll(mode_one, LANES - g * NI, 1) for g in range(8)], axis=0
    )
    a_t = jnp.dot(h_inv[...], mode_one_t, precision=HIGHEST, preferred_element_type=F32)
    for i in range(NI):
        a_wide[i] = jnp.broadcast_to(a_t[:, i : i + 1], (R, LANES))

    def combine(tiles):
        accs = [partial[tile, 0] * a_wide[0] for tile in tiles]
        for i in range(1, NI):
            wide_a = a_wide[i]
            accs = [acc + partial[tile, i] * wide_a for acc, tile in zip(accs, tiles)]
        return accs

    order = (2, 1, 3, 0)

    def tiles_of(dy, to_core):
        return [(to_zhi * NY + (y + dy) % NY) * 2 + to_core for to_zhi in range(2)]

    pair_copies = [
        remote(pair_send.at[n], pair_recv.at[n], pair_ssem.at[n], pair_rsem.at[n], other_core) for n in range(NY)
    ]
    for n, dy in enumerate(order):
        for to_zhi, value in enumerate(combine(tiles_of(dy, 1 - core))):
            pair_send[n, to_zhi] = value
        pair_copies[n].start()

    lane16 = lax.broadcasted_iota(jnp.int32, (16, LANES), 1) // 32
    near_copies, far_targets = [], []
    for n, dy in enumerate(order):
        values = combine(tiles_of(dy, core))
        pair_copies[n].wait_recv()
        for to_zhi in range(2):
            value = values[to_zhi] + pair_recv[n, to_zhi]
            for to_zlo in range(NZLO):
                block = value[0:16] if to_zlo == 0 else pltpu.roll(value[0:16], LANES - 32 * to_zlo, 1)
                for g in range(1, 4):
                    piece = value[g * 16 : (g + 1) * 16]
                    shift = (32 * (g - to_zlo)) % LANES
                    block = jnp.where(lane16 == g, pltpu.roll(piece, shift, 1) if shift else piece, block)
                packed[dy, (to_zhi * NZLO + to_zlo + WITHIN + NZ - z) % NZ] = block
        if dy:
            near = remote(
                packed.at[dy, pl.ds(0, NEAR)],
                near_recv.at[n],
                near_send.at[n],
                near_rsem.at[n],
                place(x, (y + dy) % NY, z, core),
            )
            near.start()
            near_copies.append(near)
        for e in range(NEAR, NZ):
            slot = n * (NZ - NEAR) + e - NEAR
            target = place(x, (y + dy) % NY, (z + e - WITHIN) % NZ, core)
            remote(packed.at[dy, e], far_recv.at[slot], far_send, far_rsem, target).start()

    a_rows[...] = a_t.T
    a_out[...] = a_rows[pl.ds(x * NZLO + zlo, 1), :]

    for copy in near_copies:
        copy.wait_recv()
    for e in range(NEAR):
        near_sum[e] = packed[0, e] + near_recv[0, e] + near_recv[1, e] + near_recv[2, e]
    last = [e for d in range(WITHIN, 0, -1) for e in (WITHIN + d, WITHIN - d)]
    last_copies = [
        remote(near_sum.at[e], last_recv.at[n], last_send.at[n], last_rsem.at[n], at_z(e - WITHIN))
        for n, e in enumerate(last)
    ]
    for copy in last_copies:
        copy.start()

    total = near_sum[WITHIN]
    pltpu.make_async_copy(far_recv, far_recv, far_rsem).wait()
    for n in range(NY * (NZ - NEAR)):
        total = total + far_recv[n]
    for n, copy in enumerate(last_copies):
        copy.wait_recv()
        total = total + last_recv[n]
    columns = jnp.concatenate([total if g == 0 else pltpu.roll(total, LANES - 32 * g, 1) for g in range(4)], axis=0)
    two_out[...] = columns.T[0:32]

    for copy in b_copies + swap_copies + gx_copies + gz_copies + [g_swap]:
        copy.wait_send()
    pltpu.make_async_copy(one_recv, one_recv, one_send).wait()

    for copy in pair_copies + near_copies + last_copies:
        copy.wait_send()
    pltpu.make_async_copy(far_recv, far_recv, far_send).wait()


def body(tensor, factor_b, factor_c):
    dma = pltpu.SemaphoreType.DMA
    vmem = pl.BlockSpec(memory_space=pltpu.VMEM)
    hbm = pl.BlockSpec(memory_space=pltpu.HBM)
    a_rows, two = pl.pallas_call(
        kernel,
        name="cp_step",
        out_shape=(jax.ShapeDtypeStruct((1, R), F32), jax.ShapeDtypeStruct((32, R), F32)),
        in_specs=[hbm, hbm, hbm],
        out_specs=(vmem, vmem),
        scratch_shapes=[
            pltpu.VMEM((R, 512), F32),
            pltpu.VMEM((NK, R), F32),
            pltpu.VMEM((NI, NK, NT * LANES), F32),
            pltpu.VMEM((NT, NI, R, LANES), F32),
            pltpu.VMEM((4 * R, 4 * NK), BF16),
            pltpu.VMEM((R, LANES), F32),
            pltpu.VMEM((3, R // 2, LANES), F32),
            pltpu.VMEM((R // 2, LANES), F32),
            pltpu.VMEM((3, R // 2, LANES), F32),
            pltpu.VMEM((R, LANES), F32),
            pltpu.VMEM((3, R, 512), F32),
            pltpu.VMEM((NI, R, LANES), F32),
            pltpu.VMEM((8, LANES), F32),
            pltpu.VMEM((15, 8, LANES), F32),
            pltpu.VMEM((R, R), F32),
            pltpu.VMEM((NI, R, LANES), F32),
            pltpu.VMEM((LANES, R), F32),
            pltpu.VMEM((NY, 2, R, LANES), F32),
            pltpu.VMEM((NY, 2, R, LANES), F32),
            pltpu.VMEM((NY, NZ, 16, LANES), F32),
            pltpu.VMEM((NY - 1, NEAR, 16, LANES), F32),
            pltpu.VMEM((NEAR, 16, LANES), F32),
            pltpu.VMEM((NEAR - 1, 16, LANES), F32),
            pltpu.VMEM((NY * (NZ - NEAR), 16, LANES), F32),
            dma((2,)),
            dma((NI,)),
            dma((7,)),
            dma((7,)),
            dma((3,)),
            dma((3,)),
            dma((3,)),
            dma((3,)),
            dma,
            dma,
            dma,
            dma,
            dma((NY,)),
            dma((NY,)),
            dma((NY - 1,)),
            dma((NY - 1,)),
            dma((NEAR - 1,)),
            dma((NEAR - 1,)),
            dma,
            dma,
        ],
        compiler_params=pltpu.CompilerParams(collective_id=0, has_side_effects=True, vmem_limit_bytes=48 * 2**20),
        cost_estimate=pl.CostEstimate(flops=2**30, bytes_accessed=2**23, transcendentals=0),
    )(
        tensor,
        pltpu.with_memory_space_constraint(factor_b.T, pltpu.HBM),
        pltpu.with_memory_space_constraint(factor_c, pltpu.HBM),
    )
    return a_rows, two.T.reshape(R, 1, 32)


def solution(mesh):
    placed = (P("ia", "ka", "ja"), P(("ja", "ka"), None), P("ka", None))
    return jax.shard_map(
        body,
        mesh=mesh,
        in_specs=placed,
        out_specs=(P(("ia", "ja", "ka"), None), P(None, "ja", ("ia", "ka"))),
        check_vma=False,
    )
```

```python
import jax
import jax.numpy as jnp
from jax import lax
from jax.experimental import pallas as pl
from jax.experimental.pallas import tpu as pltpu
from jax.sharding import PartitionSpec as P

MESH = pl.DeviceIdType.MESH
F32 = jnp.float32
BF16 = jnp.bfloat16
HIGHEST = lax.Precision.HIGHEST

R = 64
NI = 16
NK = 64
NT = 16
LANES = 128
NX, NY, NZ, NZLO = 4, 4, 8, 4
WITHIN = 2
NEAR = 2 * WITHIN + 1


def place(x, y, z, core):
    return (((z // NZLO) * NY + y) * 2 + core, x, z % NZLO)


def kernel(
    tensor,
    b_hbm,
    c_hbm,
    a_out,
    two_out,
    b_ref,
    c_ref,
    rows,
    partial,
    c_wide,
    gram_own,
    gram_x,
    gram_mid,
    gram_z,
    gram_sum,
    b_in,
    one_acc,
    one_own,
    one_recv,
    h_inv,
    a_wide,
    a_rows,
    pair_send,
    pair_recv,
    packed,
    near_recv,
    near_sum,
    last_recv,
    far_recv,
    in_sem,
    t_sem,
    b_send,
    b_recv_sem,
    gx_send,
    gx_recv,
    gz_send,
    gz_recv,
    gs_send,
    gs_recv,
    one_send,
    one_recv_sem,
    pair_ssem,
    pair_rsem,
    near_send,
    near_rsem,
    last_send,
    last_rsem,
    far_send,
    far_rsem,
):
    ia = lax.axis_index("ia")
    x = lax.axis_index("ja")
    zlo = lax.axis_index("ka")
    core = ia % 2
    y = (ia // 2) % NY
    zhi = ia // (2 * NY)
    z = zhi * NZLO + zlo

    xs = [x] + [lax.rem(x + d, NX) for d in range(1, NX)]
    zlos = [zlo] + [lax.rem(zlo + d, NZLO) for d in range(1, NZLO)]

    def at_z(d):
        return place(x, y, (z + d + NZ) % NZ, core)

    def at_x(d):
        return place((x + d) % NX, y, z, core)

    other_core = place(x, y, z, 1 - core)

    def remote(src, dst, send, recv, target):
        copy = pltpu.make_async_remote_copy(
            src_ref=src, dst_ref=dst, send_sem=send, recv_sem=recv, device_id=target, device_id_type=MESH
        )
        return copy

    def load_row(i):
        return pltpu.make_async_copy(tensor.at[i], rows.at[i], t_sem.at[i])

    load_c = pltpu.make_async_copy(c_hbm, c_ref, in_sem.at[0])
    load_b = pltpu.make_async_copy(b_hbm, b_ref, in_sem.at[1])
    load_c.start()
    load_b.start()
    for i in range(NI):
        load_row(i).start()

    barrier = pltpu.get_barrier_semaphore()
    peers = [other_core]
    peers += [at_x(d) for d in range(1, NX)]
    peers += [place(x, (y + d) % NY, z, core) for d in range(1, NY)]
    peers += [at_z(d) for d in range(1, NZ)]
    for peer in peers:
        pl.semaphore_signal(barrier, inc=1, device_id=peer, device_id_type=MESH)

    load_c.wait()
    c_t = c_ref[...].T
    c_hi = c_t.astype(BF16)
    c_lo = (c_t - c_hi.astype(F32)).astype(BF16)
    none = jnp.zeros_like(c_hi)
    for n, part in enumerate((c_hi, c_lo)):
        c_wide[n * 2 * R : n * 2 * R + R] = jnp.concatenate([part, part, none, none], axis=1)
        c_wide[n * 2 * R + R : (n + 1) * 2 * R] = jnp.concatenate([none, none, part, part], axis=1)
    def contract(i, carry):
        load_row(2 * i).wait()
        load_row(2 * i + 1).wait()
        for chunk in range(8):
            operand = []
            for n in range(2):
                values = rows[2 * i + n, :, pl.ds(chunk * 256, 256)]
                hi = values.astype(BF16)
                operand += [hi, (values - hi.astype(F32)).astype(BF16)]
            out = jnp.dot(c_wide[...], jnp.concatenate(operand, axis=0), preferred_element_type=F32)
            out = out[: 2 * R] + out[2 * R :]
            for part in range(2):
                for n in range(2):
                    piece = out[n * R : (n + 1) * R, part * LANES : (part + 1) * LANES]
                    partial[chunk * 2 + part, 2 * i + n] = piece
        return carry

    load_b.wait()
    pl.semaphore_wait(barrier, len(peers))

    half = b_ref.shape[1] // 2
    own_half = pl.ds(pl.multiple_of(core * half, half), half)
    quarters = [pl.ds(pl.multiple_of(core * half + n * half // 2, half // 2), half // 2) for n in range(2)]
    far_copies = [
        remote(b_ref.at[:, quarters[n]], b_in.at[2, :, quarters[n]], b_send.at[2 + n], b_recv_sem.at[2 + n], at_z(d))
        for n, d in enumerate((2, -2))
    ]
    near_b_copies = [
        remote(b_ref.at[:, own_half], b_in.at[n, :, own_half], b_send.at[n], b_recv_sem.at[n], at_z(d))
        for n, d in enumerate((1, -1))
    ]
    swap_copies = [
        remote(b_in.at[n, :, own_half], b_in.at[n, :, own_half], b_send.at[4 + n], b_recv_sem.at[4 + n], other_core)
        for n in range(3)
    ]
    b_copies = far_copies + near_b_copies
    for copy in b_copies:
        copy.start()

    b_own = b_ref[...]
    gram_b = lax.dot_general(b_own, b_own, (((1,), (1,)), ((), ())), precision=HIGHEST, preferred_element_type=F32)
    gram_c = lax.dot_general(c_t, c_t, (((1,), (1,)), ((), ())), precision=HIGHEST, preferred_element_type=F32)
    gram_own[...] = jnp.concatenate([gram_b, gram_c], axis=1)

    own_rows = pl.ds(pl.multiple_of(core * (R // 2), R // 2), R // 2)
    gx_copies = [remote(gram_own.at[own_rows], gram_x.at[d - 1], gx_send.at[d - 1], gx_recv.at[d - 1], at_x(d)) for d in (2, 1, 3)]
    for copy in gx_copies:
        copy.start()

    lax.fori_loop(0, NI // 2, contract, 0, unroll=2)

    for copy in gx_copies:
        copy.wait_recv()
    own = gram_own[own_rows, :]
    total = own + gram_x[0] + gram_x[1] + gram_x[2]
    gram_mid[...] = jnp.where(lax.broadcasted_iota(jnp.int32, (R // 2, LANES), 1) < R, total, own)
    gz_copies = [
        remote(gram_mid, gram_z.at[n], gz_send.at[n], gz_recv.at[n], at_z(d)) for n, d in enumerate((2, 1, -1))
    ]
    for copy in gz_copies:
        copy.start()

    def first_block(i, carry):
        acc = jnp.zeros((R, LANES), F32)
        for part in range(4):
            acc += partial[zlo * 4 + part, i] * b_ref[:, part * LANES : (part + 1) * LANES]
        one_acc[i] = acc
        return carry

    lax.fori_loop(0, NI, first_block, 0, unroll=4)

    for copy in far_copies:
        copy.wait_recv()
    swap_copies[2].start()
    for n in range(2):
        near_b_copies[n].wait_recv()
        swap_copies[n].start()
    blocks = ((zlo + 3) % NZLO, (zlo + 1) % NZLO, (zlo + 2) % NZLO)

    def half_blocks(i, to_core):
        acc = one_acc[i]
        for n in range(3):
            for part in range(2):
                start = pl.multiple_of(to_core * half + part * LANES, LANES)
                acc += partial[blocks[n] * 4 + to_core * 2 + part, i] * b_in[n, :, pl.ds(start, LANES)]
        return acc

    def fetched_half(i, carry):
        one_acc[i] = half_blocks(i, core)
        return carry

    lax.fori_loop(0, NI, fetched_half, 0, unroll=4)

    for copy in swap_copies:
        copy.wait_recv()
    lane8 = lax.broadcasted_iota(jnp.int32, (8, LANES), 1)

    def handed_half(i, carry):
        acc = half_blocks(i, 1 - core)
        for g in range(8):
            total = jnp.sum(acc[g * 8 : (g + 1) * 8], axis=1, keepdims=True)
            carry = jnp.where(lane8 == g * NI + i, total, carry)
        return carry

    one_own[...] = lax.fori_loop(0, NI, handed_half, jnp.zeros((8, LANES), F32), unroll=4)

    one_targets = [(dx, dz) for dz in (3, 1, 2) for dx in (2, 1, 3)] + [(0, 3), (0, 1), (2, 0), (0, 2), (1, 0), (3, 0)]
    for n, (dx, dz) in enumerate(one_targets):
        target = (ia, xs[dx], zlos[dz])
        remote(one_own, one_recv.at[n], one_send, one_recv_sem, target).start()

    for copy in gz_copies:
        copy.wait_recv()
    gram_sum[own_rows, :] = gram_mid[...] + gram_z[0] + gram_z[1] + gram_z[2]
    g_swap = remote(gram_sum.at[own_rows], gram_sum.at[own_rows], gs_send, gs_recv, other_core)
    g_swap.start()
    g_swap.wait_recv()
    grams = gram_sum[...]
    lane = lax.broadcasted_iota(jnp.int32, (R, LANES), 1)
    product = grams * pltpu.roll(grams, R, 1)
    row_id = lax.broadcasted_iota(jnp.int32, (R, LANES), 0)
    work = jnp.where(lane < R, product, jnp.where(lane == row_id + R, 1.0, 0.0))
    groups = [work[g * 8 : (g + 1) * 8] for g in range(8)]

    def wide(value):
        return jnp.broadcast_to(value, (8, LANES))

    sub = lax.broadcasted_iota(jnp.int32, (8, LANES), 0)
    for p in range(8):
        columns = {g: [wide(groups[g][:, p * 8 + j : p * 8 + j + 1]) for j in range(8)] for g in range(p, 8)}
        block = [[wide(columns[p][j][i : i + 1]) for j in range(i + 1)] for i in range(8)]
        scale = []
        for j in range(8):
            scale.append(lax.rsqrt(block[j][j]))
            for i in range(j + 1, 8):
                block[i][j] = block[i][j] * scale[j]
            for i in range(j + 1, 8):
                for k in range(j + 1, i + 1):
                    block[i][k] = block[i][k] - block[i][j] * block[k][j]
        units = []
        for j in range(8):
            unit = wide(groups[p][j : j + 1])
            for k in range(j):
                unit = unit - block[j][k] * units[k]
            units.append(unit * scale[j])
        done = units[0]
        for j in range(1, 8):
            done = jnp.where(sub == j, units[j], done)
        groups[p] = done
        for g in range(p + 1, 8):
            lower = []
            for j in range(8):
                column = columns[g][j]
                for k in range(j):
                    column = column - lower[k] * block[j][k]
                lower.append(column * scale[j])
                groups[g] = groups[g] - lower[j] * units[j]
    lower_inv = jnp.concatenate(groups, axis=0)[:, R:]
    h_inv[...] = lax.dot_general(
        lower_inv, lower_inv, (((0,), (0,)), ((), ())), precision=HIGHEST, preferred_element_type=F32
    )

    pltpu.make_async_copy(one_recv, one_recv, one_recv_sem).wait()
    mode_one = one_own[...]
    for n in range(NX * NZLO - 1):
        mode_one = mode_one + one_recv[n]
    mode_one_t = jnp.concatenate(
        [mode_one if g == 0 else pltpu.roll(mode_one, LANES - g * NI, 1) for g in range(8)], axis=0
    )
    a_t = jnp.dot(h_inv[...], mode_one_t, precision=HIGHEST, preferred_element_type=F32)
    for i in range(NI):
        a_wide[i] = jnp.broadcast_to(a_t[:, i : i + 1], (R, LANES))

    def combine(tiles):
        accs = [partial[tile, 0] * a_wide[0] for tile in tiles]
        for i in range(1, NI):
            wide_a = a_wide[i]
            accs = [acc + partial[tile, i] * wide_a for acc, tile in zip(accs, tiles)]
        return accs

    order = (2, 1, 3, 0)

    def tiles_of(dy, to_core):
        return [(to_zhi * NY + (y + dy) % NY) * 2 + to_core for to_zhi in range(2)]

    pair_copies = [
        remote(pair_send.at[n], pair_recv.at[n], pair_ssem.at[n], pair_rsem.at[n], other_core) for n in range(NY)
    ]
    for n, dy in enumerate(order):
        for to_zhi, value in enumerate(combine(tiles_of(dy, 1 - core))):
            pair_send[n, to_zhi] = value
        pair_copies[n].start()

    lane16 = lax.broadcasted_iota(jnp.int32, (16, LANES), 1) // 32
    near_copies, far_targets = [], []
    for n, dy in enumerate(order):
        values = combine(tiles_of(dy, core))
        pair_copies[n].wait_recv()
        for to_zhi in range(2):
            value = values[to_zhi] + pair_recv[n, to_zhi]
            for to_zlo in range(NZLO):
                block = value[0:16] if to_zlo == 0 else pltpu.roll(value[0:16], LANES - 32 * to_zlo, 1)
                for g in range(1, 4):
                    piece = value[g * 16 : (g + 1) * 16]
                    shift = (32 * (g - to_zlo)) % LANES
                    block = jnp.where(lane16 == g, pltpu.roll(piece, shift, 1) if shift else piece, block)
                packed[dy, (to_zhi * NZLO + to_zlo + WITHIN + NZ - z) % NZ] = block
        if dy:
            near = remote(
                packed.at[dy, pl.ds(0, NEAR)],
                near_recv.at[n],
                near_send.at[n],
                near_rsem.at[n],
                place(x, (y + dy) % NY, z, core),
            )
            near.start()
            near_copies.append(near)
        for e in range(NEAR, NZ):
            slot = n * (NZ - NEAR) + e - NEAR
            target = place(x, (y + dy) % NY, (z + e - WITHIN) % NZ, core)
            remote(packed.at[dy, e], far_recv.at[slot], far_send, far_rsem, target).start()

    a_rows[...] = a_t.T
    a_out[...] = a_rows[pl.ds(x * NZLO + zlo, 1), :]

    for copy in near_copies:
        copy.wait_recv()
    for e in range(NEAR):
        near_sum[e] = packed[0, e] + near_recv[0, e] + near_recv[1, e] + near_recv[2, e]
    last = [e for d in range(WITHIN, 0, -1) for e in (WITHIN + d, WITHIN - d)]
    last_copies = [
        remote(near_sum.at[e], last_recv.at[n], last_send.at[n], last_rsem.at[n], at_z(e - WITHIN))
        for n, e in enumerate(last)
    ]
    for copy in last_copies:
        copy.start()

    total = near_sum[WITHIN]
    pltpu.make_async_copy(far_recv, far_recv, far_rsem).wait()
    for n in range(NY * (NZ - NEAR)):
        total = total + far_recv[n]
    for n, copy in enumerate(last_copies):
        copy.wait_recv()
        total = total + last_recv[n]
    columns = jnp.concatenate([total if g == 0 else pltpu.roll(total, LANES - 32 * g, 1) for g in range(4)], axis=0)
    two_out[...] = columns.T[0:32]

    for copy in b_copies + swap_copies + gx_copies + gz_copies + [g_swap]:
        copy.wait_send()
    pltpu.make_async_copy(one_recv, one_recv, one_send).wait()

    for copy in pair_copies + near_copies + last_copies:
        copy.wait_send()
    pltpu.make_async_copy(far_recv, far_recv, far_send).wait()


def body(tensor, factor_b, factor_c):
    dma = pltpu.SemaphoreType.DMA
    vmem = pl.BlockSpec(memory_space=pltpu.VMEM)
    hbm = pl.BlockSpec(memory_space=pltpu.HBM)
    a_rows, two = pl.pallas_call(
        kernel,
        name="cp_step",
        out_shape=(jax.ShapeDtypeStruct((1, R), F32), jax.ShapeDtypeStruct((32, R), F32)),
        in_specs=[hbm, hbm, hbm],
        out_specs=(vmem, vmem),
        scratch_shapes=[
            pltpu.VMEM((R, 512), F32),
            pltpu.VMEM((NK, R), F32),
            pltpu.VMEM((NI, NK, NT * LANES), F32),
            pltpu.VMEM((NT, NI, R, LANES), F32),
            pltpu.VMEM((4 * R, 4 * NK), BF16),
            pltpu.VMEM((R, LANES), F32),
            pltpu.VMEM((3, R // 2, LANES), F32),
            pltpu.VMEM((R // 2, LANES), F32),
            pltpu.VMEM((3, R // 2, LANES), F32),
            pltpu.VMEM((R, LANES), F32),
            pltpu.VMEM((3, R, 512), F32),
            pltpu.VMEM((NI, R, LANES), F32),
            pltpu.VMEM((8, LANES), F32),
            pltpu.VMEM((15, 8, LANES), F32),
            pltpu.VMEM((R, R), F32),
            pltpu.VMEM((NI, R, LANES), F32),
            pltpu.VMEM((LANES, R), F32),
            pltpu.VMEM((NY, 2, R, LANES), F32),
            pltpu.VMEM((NY, 2, R, LANES), F32),
            pltpu.VMEM((NY, NZ, 16, LANES), F32),
            pltpu.VMEM((NY - 1, NEAR, 16, LANES), F32),
            pltpu.VMEM((NEAR, 16, LANES), F32),
            pltpu.VMEM((NEAR - 1, 16, LANES), F32),
            pltpu.VMEM((NY * (NZ - NEAR), 16, LANES), F32),
            dma((2,)),
            dma((NI,)),
            dma((7,)),
            dma((7,)),
            dma((3,)),
            dma((3,)),
            dma((3,)),
            dma((3,)),
            dma,
            dma,
            dma,
            dma,
            dma((NY,)),
            dma((NY,)),
            dma((NY - 1,)),
            dma((NY - 1,)),
            dma((NEAR - 1,)),
            dma((NEAR - 1,)),
            dma,
            dma,
        ],
        compiler_params=pltpu.CompilerParams(collective_id=0, has_side_effects=True, vmem_limit_bytes=48 * 2**20),
        cost_estimate=pl.CostEstimate(flops=2**30, bytes_accessed=2**23, transcendentals=0),
    )(
        tensor,
        pltpu.with_memory_space_constraint(factor_b.T, pltpu.HBM),
        pltpu.with_memory_space_constraint(factor_c, pltpu.HBM),
    )
    return a_rows, two.T.reshape(R, 1, 32)


def solution(mesh):
    placed = (P("ia", "ka", "ja"), P(("ja", "ka"), None), P("ka", None))
    return jax.shard_map(
        body,
        mesh=mesh,
        in_specs=placed,
        out_specs=(P(("ia", "ja", "ka"), None), P(None, "ja", ("ia", "ka"))),
        check_vma=False,
    )
```

```python
import jax
import jax.numpy as jnp
from jax import lax
from jax.experimental import pallas as pl
from jax.experimental.pallas import tpu as pltpu
from jax.sharding import PartitionSpec as P

MESH = pl.DeviceIdType.MESH
F32 = jnp.float32
BF16 = jnp.bfloat16
HIGHEST = lax.Precision.HIGHEST

R = 64
NI = 16
NK = 64
NT = 16
LANES = 128
NX, NY, NZ, NZLO = 4, 4, 8, 4
WITHIN = 2
NEAR = 2 * WITHIN + 1


def place(x, y, z, core):
    return (((z // NZLO) * NY + y) * 2 + core, x, z % NZLO)


def kernel(
    tensor,
    b_hbm,
    c_hbm,
    a_out,
    two_out,
    b_ref,
    c_ref,
    rows,
    partial,
    c_wide,
    gram_own,
    gram_x,
    gram_mid,
    gram_z,
    gram_sum,
    b_in,
    one_acc,
    one_own,
    one_recv,
    h_inv,
    a_wide,
    a_rows,
    pair_send,
    pair_recv,
    packed,
    near_recv,
    near_sum,
    last_recv,
    far_recv,
    in_sem,
    t_sem,
    b_send,
    b_recv_sem,
    gx_send,
    gx_recv,
    gz_send,
    gz_recv,
    gs_send,
    gs_recv,
    one_send,
    one_recv_sem,
    pair_ssem,
    pair_rsem,
    near_send,
    near_rsem,
    last_send,
    last_rsem,
    far_send,
    far_rsem,
):
    ia = lax.axis_index("ia")
    x = lax.axis_index("ja")
    zlo = lax.axis_index("ka")
    core = ia % 2
    y = (ia // 2) % NY
    zhi = ia // (2 * NY)
    z = zhi * NZLO + zlo

    xs = [x] + [lax.rem(x + d, NX) for d in range(1, NX)]
    zlos = [zlo] + [lax.rem(zlo + d, NZLO) for d in range(1, NZLO)]

    ys = [y] + [lax.rem(y + d, NY) for d in range(1, NY)]
    zs = [z] + [lax.rem(z + d, NZ) for d in range(1, NZ)]
    zhis = [lax.div(v, NZLO) for v in zs]
    zls = [lax.rem(v, NZLO) for v in zs]

    def at_z(d):
        return place(x, y, (z + d + NZ) % NZ, core)

    def at_x(d):
        return place((x + d) % NX, y, z, core)

    other_core = place(x, y, z, 1 - core)

    def remote(src, dst, send, recv, target):
        copy = pltpu.make_async_remote_copy(
            src_ref=src, dst_ref=dst, send_sem=send, recv_sem=recv, device_id=target, device_id_type=MESH
        )
        return copy

    def load_row(i):
        return pltpu.make_async_copy(tensor.at[i], rows.at[i], t_sem.at[i])

    load_c = pltpu.make_async_copy(c_hbm, c_ref, in_sem.at[0])
    load_b = pltpu.make_async_copy(b_hbm, b_ref, in_sem.at[1])
    load_c.start()
    load_b.start()
    for i in range(NI):
        load_row(i).start()

    barrier = pltpu.get_barrier_semaphore()
    peers = [other_core]
    peers += [at_x(d) for d in range(1, NX)]
    peers += [place(x, (y + d) % NY, z, core) for d in range(1, NY)]
    peers += [at_z(d) for d in range(1, NZ)]
    for peer in peers:
        pl.semaphore_signal(barrier, inc=1, device_id=peer, device_id_type=MESH)

    def contract(i, carry):
        load_row(2 * i).wait()
        load_row(2 * i + 1).wait()
        for chunk in range(8):
            operand = []
            for n in range(2):
                values = rows[2 * i + n, :, pl.ds(chunk * 256, 256)]
                hi = values.astype(BF16)
                operand += [hi, (values - hi.astype(F32)).astype(BF16)]
            out = jnp.dot(c_wide[...], jnp.concatenate(operand, axis=0), preferred_element_type=F32)
            out = out[: 2 * R] + out[2 * R :]
            for part in range(2):
                for n in range(2):
                    piece = out[n * R : (n + 1) * R, part * LANES : (part + 1) * LANES]
                    partial[chunk * 2 + part, 2 * i + n] = piece
        return carry

    load_b.wait()
    pl.semaphore_wait(barrier, len(peers))

    half = b_ref.shape[1] // 2
    own_half = pl.ds(pl.multiple_of(core * half, half), half)
    quarters = [pl.ds(pl.multiple_of(core * half + n * half // 2, half // 2), half // 2) for n in range(2)]
    far_copies = [
        remote(b_ref.at[:, quarters[n]], b_in.at[2, :, quarters[n]], b_send.at[2 + n], b_recv_sem.at[2 + n], at_z(d))
        for n, d in enumerate((2, -2))
    ]
    near_b_copies = [
        remote(b_ref.at[:, own_half], b_in.at[n, :, own_half], b_send.at[n], b_recv_sem.at[n], at_z(d))
        for n, d in enumerate((1, -1))
    ]
    swap_copies = [
        remote(b_in.at[n, :, own_half], b_in.at[n, :, own_half], b_send.at[4 + n], b_recv_sem.at[4 + n], other_core)
        for n in range(3)
    ]
    b_copies = far_copies + near_b_copies
    for copy in b_copies:
        copy.start()

    load_c.wait()
    c_t = c_ref[...].T
    c_hi = c_t.astype(BF16)
    c_lo = (c_t - c_hi.astype(F32)).astype(BF16)
    none = jnp.zeros_like(c_hi)
    for n, part in enumerate((c_hi, c_lo)):
        c_wide[n * 2 * R : n * 2 * R + R] = jnp.concatenate([part, part, none, none], axis=1)
        c_wide[n * 2 * R + R : (n + 1) * 2 * R] = jnp.concatenate([none, none, part, part], axis=1)
    b_own = b_ref[...]
    gram_b = lax.dot_general(b_own, b_own, (((1,), (1,)), ((), ())), precision=HIGHEST, preferred_element_type=F32)
    gram_c = lax.dot_general(c_t, c_t, (((1,), (1,)), ((), ())), precision=HIGHEST, preferred_element_type=F32)
    gram_own[...] = jnp.concatenate([gram_b, gram_c], axis=1)

    own_rows = pl.ds(pl.multiple_of(core * (R // 2), R // 2), R // 2)
    gx_copies = [remote(gram_own.at[own_rows], gram_x.at[d - 1], gx_send.at[d - 1], gx_recv.at[d - 1], at_x(d)) for d in (2, 1, 3)]
    for copy in gx_copies:
        copy.start()

    lax.fori_loop(0, NI // 2, contract, 0, unroll=2)

    for copy in gx_copies:
        copy.wait_recv()
    own = gram_own[own_rows, :]
    total = own + gram_x[0] + gram_x[1] + gram_x[2]
    gram_mid[...] = jnp.where(lax.broadcasted_iota(jnp.int32, (R // 2, LANES), 1) < R, total, own)
    gz_copies = [
        remote(gram_mid, gram_z.at[n], gz_send.at[n], gz_recv.at[n], at_z(d)) for n, d in enumerate((2, 1, -1))
    ]
    for copy in gz_copies:
        copy.start()

    def first_block(i, carry):
        acc = jnp.zeros((R, LANES), F32)
        for part in range(4):
            acc += partial[zlo * 4 + part, i] * b_ref[:, part * LANES : (part + 1) * LANES]
        one_acc[i] = acc
        return carry

    lax.fori_loop(0, NI, first_block, 0, unroll=8)

    for copy in far_copies:
        copy.wait_recv()
    swap_copies[2].start()
    for n in range(2):
        near_b_copies[n].wait_recv()
        swap_copies[n].start()
    blocks = ((zlo + 3) % NZLO, (zlo + 1) % NZLO, (zlo + 2) % NZLO)

    def half_blocks(i, to_core):
        acc = one_acc[i]
        for n in range(3):
            for part in range(2):
                start = pl.multiple_of(to_core * half + part * LANES, LANES)
                acc += partial[blocks[n] * 4 + to_core * 2 + part, i] * b_in[n, :, pl.ds(start, LANES)]
        return acc

    def fetched_half(i, carry):
        one_acc[i] = half_blocks(i, core)
        return carry

    lax.fori_loop(0, NI, fetched_half, 0, unroll=8)

    for copy in swap_copies:
        copy.wait_recv()
    lane8 = lax.broadcasted_iota(jnp.int32, (8, LANES), 1)

    def handed_half(i, carry):
        acc = half_blocks(i, 1 - core)
        for g in range(8):
            total = jnp.sum(acc[g * 8 : (g + 1) * 8], axis=1, keepdims=True)
            carry = jnp.where(lane8 == g * NI + i, total, carry)
        return carry

    one_own[...] = lax.fori_loop(0, NI, handed_half, jnp.zeros((8, LANES), F32), unroll=8)

    one_targets = [(dx, dz) for dz in (3, 1, 2) for dx in (2, 1, 3)] + [(0, 3), (0, 1), (2, 0), (0, 2), (1, 0), (3, 0)]
    for n, (dx, dz) in enumerate(one_targets):
        target = (ia, xs[dx], zlos[dz])
        remote(one_own, one_recv.at[n], one_send, one_recv_sem, target).start()

    for copy in gz_copies:
        copy.wait_recv()
    gram_sum[own_rows, :] = gram_mid[...] + gram_z[0] + gram_z[1] + gram_z[2]
    g_swap = remote(gram_sum.at[own_rows], gram_sum.at[own_rows], gs_send, gs_recv, other_core)
    g_swap.start()
    g_swap.wait_recv()
    grams = gram_sum[...]
    lane = lax.broadcasted_iota(jnp.int32, (R, LANES), 1)
    product = grams * pltpu.roll(grams, R, 1)
    row_id = lax.broadcasted_iota(jnp.int32, (R, LANES), 0)
    work = jnp.where(lane < R, product, jnp.where(lane == row_id + R, 1.0, 0.0))
    groups = [work[g * 8 : (g + 1) * 8] for g in range(8)]

    def wide(value):
        return jnp.broadcast_to(value, (8, LANES))

    sub = lax.broadcasted_iota(jnp.int32, (8, LANES), 0)
    for p in range(8):
        columns = {g: [wide(groups[g][:, p * 8 + j : p * 8 + j + 1]) for j in range(8)] for g in range(p, 8)}
        block = [[wide(columns[p][j][i : i + 1]) for j in range(i + 1)] for i in range(8)]
        scale = []
        for j in range(8):
            scale.append(lax.rsqrt(block[j][j]))
            for i in range(j + 1, 8):
                block[i][j] = block[i][j] * scale[j]
            for i in range(j + 1, 8):
                for k in range(j + 1, i + 1):
                    block[i][k] = block[i][k] - block[i][j] * block[k][j]
        units = []
        for j in range(8):
            unit = wide(groups[p][j : j + 1])
            for k in range(j):
                unit = unit - block[j][k] * units[k]
            units.append(unit * scale[j])
        done = units[0]
        for j in range(1, 8):
            done = jnp.where(sub == j, units[j], done)
        groups[p] = done
        for g in range(p + 1, 8):
            lower = []
            for j in range(8):
                column = columns[g][j]
                for k in range(j):
                    column = column - lower[k] * block[j][k]
                lower.append(column * scale[j])
                groups[g] = groups[g] - lower[j] * units[j]
    lower_inv = jnp.concatenate(groups, axis=0)[:, R:]
    h_inv[...] = lax.dot_general(
        lower_inv, lower_inv, (((0,), (0,)), ((), ())), precision=HIGHEST, preferred_element_type=F32
    )

    pltpu.make_async_copy(one_recv, one_recv, one_recv_sem).wait()
    mode_one = one_own[...]
    for n in range(NX * NZLO - 1):
        mode_one = mode_one + one_recv[n]
    mode_one_t = jnp.concatenate(
        [mode_one if g == 0 else pltpu.roll(mode_one, LANES - g * NI, 1) for g in range(8)], axis=0
    )
    a_t = jnp.dot(h_inv[...], mode_one_t, precision=HIGHEST, preferred_element_type=F32)
    for i in range(NI):
        a_wide[i] = jnp.broadcast_to(a_t[:, i : i + 1], (R, LANES))

    def combine(tiles):
        accs = [partial[tile, 0] * a_wide[0] for tile in tiles]
        for i in range(1, NI):
            wide_a = a_wide[i]
            accs = [acc + partial[tile, i] * wide_a for acc, tile in zip(accs, tiles)]
        return accs

    order = (2, 1, 3, 0)

    def tiles_of(dy, to_core):
        return [(to_zhi * NY + ys[dy]) * 2 + to_core for to_zhi in range(2)]

    pair_copies = [
        remote(pair_send.at[n], pair_recv.at[n], pair_ssem.at[n], pair_rsem.at[n], other_core) for n in range(NY)
    ]
    for n, dy in enumerate(order):
        for to_zhi, value in enumerate(combine(tiles_of(dy, 1 - core))):
            pair_send[n, to_zhi] = value
        pair_copies[n].start()

    lane16 = lax.broadcasted_iota(jnp.int32, (16, LANES), 1) // 32
    near_copies, far_targets = [], []
    for n, dy in enumerate(order):
        values = combine(tiles_of(dy, core))
        pair_copies[n].wait_recv()
        for to_zhi in range(2):
            value = values[to_zhi] + pair_recv[n, to_zhi]
            for to_zlo in range(NZLO):
                block = value[0:16] if to_zlo == 0 else pltpu.roll(value[0:16], LANES - 32 * to_zlo, 1)
                for g in range(1, 4):
                    piece = value[g * 16 : (g + 1) * 16]
                    shift = (32 * (g - to_zlo)) % LANES
                    block = jnp.where(lane16 == g, pltpu.roll(piece, shift, 1) if shift else piece, block)
                packed[dy, lax.rem(to_zhi * NZLO + to_zlo + WITHIN + NZ - z, NZ)] = block
        if dy:
            near = remote(
                packed.at[dy, pl.ds(0, NEAR)],
                near_recv.at[n],
                near_send.at[n],
                near_rsem.at[n],
                place(x, (y + dy) % NY, z, core),
            )
            near.start()
            near_copies.append(near)
        for e in range(NEAR, NZ):
            slot = n * (NZ - NEAR) + e - NEAR
            target = ((zhis[(e - WITHIN) % NZ] * NY + ys[dy]) * 2 + core, x, zls[(e - WITHIN) % NZ])
            remote(packed.at[dy, e], far_recv.at[slot], far_send, far_rsem, target).start()

    a_rows[...] = a_t.T
    a_out[...] = a_rows[pl.ds(x * NZLO + zlo, 1), :]

    for copy in near_copies:
        copy.wait_recv()
    for e in range(NEAR):
        near_sum[e] = packed[0, e] + near_recv[0, e] + near_recv[1, e] + near_recv[2, e]
    last = [e for d in range(WITHIN, 0, -1) for e in (WITHIN + d, WITHIN - d)]
    last_copies = [
        remote(near_sum.at[e], last_recv.at[n], last_send.at[n], last_rsem.at[n], at_z(e - WITHIN))
        for n, e in enumerate(last)
    ]
    for copy in last_copies:
        copy.start()

    total = near_sum[WITHIN]
    pltpu.make_async_copy(far_recv, far_recv, far_rsem).wait()
    for n in range(NY * (NZ - NEAR)):
        total = total + far_recv[n]
    for n, copy in enumerate(last_copies):
        copy.wait_recv()
        total = total + last_recv[n]
    columns = jnp.concatenate([total if g == 0 else pltpu.roll(total, LANES - 32 * g, 1) for g in range(4)], axis=0)
    two_out[...] = columns.T[0:32]

    for copy in b_copies + swap_copies + gx_copies + gz_copies + [g_swap]:
        copy.wait_send()
    pltpu.make_async_copy(one_recv, one_recv, one_send).wait()

    for copy in pair_copies + near_copies + last_copies:
        copy.wait_send()
    pltpu.make_async_copy(far_recv, far_recv, far_send).wait()


def body(tensor, factor_b, factor_c):
    dma = pltpu.SemaphoreType.DMA
    vmem = pl.BlockSpec(memory_space=pltpu.VMEM)
    hbm = pl.BlockSpec(memory_space=pltpu.HBM)
    a_rows, two = pl.pallas_call(
        kernel,
        name="cp_step",
        out_shape=(jax.ShapeDtypeStruct((1, R), F32), jax.ShapeDtypeStruct((32, R), F32)),
        in_specs=[hbm, hbm, hbm],
        out_specs=(vmem, vmem),
        scratch_shapes=[
            pltpu.VMEM((R, 512), F32),
            pltpu.VMEM((NK, R), F32),
            pltpu.VMEM((NI, NK, NT * LANES), F32),
            pltpu.VMEM((NT, NI, R, LANES), F32),
            pltpu.VMEM((4 * R, 4 * NK), BF16),
            pltpu.VMEM((R, LANES), F32),
            pltpu.VMEM((3, R // 2, LANES), F32),
            pltpu.VMEM((R // 2, LANES), F32),
            pltpu.VMEM((3, R // 2, LANES), F32),
            pltpu.VMEM((R, LANES), F32),
            pltpu.VMEM((3, R, 512), F32),
            pltpu.VMEM((NI, R, LANES), F32),
            pltpu.VMEM((8, LANES), F32),
            pltpu.VMEM((15, 8, LANES), F32),
            pltpu.VMEM((R, R), F32),
            pltpu.VMEM((NI, R, LANES), F32),
            pltpu.VMEM((LANES, R), F32),
            pltpu.VMEM((NY, 2, R, LANES), F32),
            pltpu.VMEM((NY, 2, R, LANES), F32),
            pltpu.VMEM((NY, NZ, 16, LANES), F32),
            pltpu.VMEM((NY - 1, NEAR, 16, LANES), F32),
            pltpu.VMEM((NEAR, 16, LANES), F32),
            pltpu.VMEM((NEAR - 1, 16, LANES), F32),
            pltpu.VMEM((NY * (NZ - NEAR), 16, LANES), F32),
            dma((2,)),
            dma((NI,)),
            dma((7,)),
            dma((7,)),
            dma((3,)),
            dma((3,)),
            dma((3,)),
            dma((3,)),
            dma,
            dma,
            dma,
            dma,
            dma((NY,)),
            dma((NY,)),
            dma((NY - 1,)),
            dma((NY - 1,)),
            dma((NEAR - 1,)),
            dma((NEAR - 1,)),
            dma,
            dma,
        ],
        compiler_params=pltpu.CompilerParams(collective_id=0, has_side_effects=True, vmem_limit_bytes=48 * 2**20),
        cost_estimate=pl.CostEstimate(flops=2**30, bytes_accessed=2**23, transcendentals=0),
    )(
        tensor,
        pltpu.with_memory_space_constraint(factor_b.T, pltpu.HBM),
        pltpu.with_memory_space_constraint(factor_c, pltpu.HBM),
    )
    return a_rows, two.T.reshape(R, 1, 32)


def solution(mesh):
    placed = (P("ia", "ka", "ja"), P(("ja", "ka"), None), P("ka", None))
    return jax.shard_map(
        body,
        mesh=mesh,
        in_specs=placed,
        out_specs=(P(("ia", "ja", "ka"), None), P(None, "ja", ("ia", "ka"))),
        check_vma=False,
    )
```
